32 devices in a mesh: dp: 8 (over y, x, core), seq: 4 (over z).
Axes of the slice: x: 2, y: 2, z: 4, core: 2. Of those that a mesh axis runs over, the one named last changes fastest.
Arguments:
- inputs: bfloat16 [8, 1024, 768], P('dp', 'seq'), may hold values from -6 to 6
- cotangent: bfloat16 [8, 1024, 768], P('dp', 'seq'), may hold values from -6 to 6
- norm1_gain: bfloat16 [2, 768], P(None, ('dp', 'seq')), may hold values from 0.5 to 1.5
- norm1_shift: bfloat16 [2, 768], P(None, ('dp', 'seq')), may hold values from -3 to 3
- query_weight: bfloat16 [2, 768, 768], P(None, ('dp', 'seq')), may hold values from -0.21875 to 0.21875
- query_bias: bfloat16 [2, 768], P(None, ('dp', 'seq')), may hold values from -3 to 3
- key_weight: bfloat16 [2, 768, 768], P(None, ('dp', 'seq')), may hold values from -0.21875 to 0.21875
- value_weight: bfloat16 [2, 768, 768], P(None, ('dp', 'seq')), may hold values from -0.21875 to 0.21875
- value_bias: bfloat16 [2, 768], P(None, ('dp', 'seq')), may hold values from -0.75 to 0.75
- out_weight: bfloat16 [2, 768, 768], P(None, ('dp', 'seq')), may hold values from -3.5 to 3.5
- out_bias: bfloat16 [2, 768], P(None, ('dp', 'seq')), may hold values from -3 to 3
- norm2_gain: bfloat16 [2, 768], P(None, ('dp', 'seq')), may hold values from 0.5 to 1.5
- norm2_shift: bfloat16 [2, 768], P(None, ('dp', 'seq')), may hold values from -3 to 3
- hidden_weight: bfloat16 [2, 768, 3072], P(None, ('dp', 'seq')), may hold values from -0.21875 to 0.21875
- hidden_bias: bfloat16 [2, 3072], P(None, ('dp', 'seq')), may hold values from -3 to 3
- proj_weight: bfloat16 [2, 3072, 768], P(None, ('dp', 'seq')), may hold values from -0.109375 to 0.109375
- proj_bias: bfloat16 [2, 768], P(None, ('dp', 'seq')), may hold values from -3 to 3
Outputs:
- outputs: bfloat16 [8, 1024, 768], P('dp', 'seq')
- grad_inputs: float32 [8, 1024, 768], P('dp', 'seq')
- grad_norm1_gain: float32 [2, 768], P(None, ('dp', 'seq'))
- grad_norm1_shift: float32 [2, 768], P(None, ('dp', 'seq'))
- grad_query_weight: float32 [2, 768, 768], P(None, ('dp', 'seq'))
- grad_query_bias: float32 [2, 768], P(None, ('dp', 'seq'))
- grad_key_weight: float32 [2, 768, 768], P(None, ('dp', 'seq'))
- grad_value_weight: float32 [2, 768, 768], P(None, ('dp', 'seq'))
- grad_value_bias: float32 [2, 768], P(None, ('dp', 'seq'))
- grad_out_weight: float32 [2, 768, 768], P(None, ('dp', 'seq'))
- grad_out_bias: float32 [2, 768], P(None, ('dp', 'seq'))
- grad_norm2_gain: float32 [2, 768], P(None, ('dp', 'seq'))
- grad_norm2_shift: float32 [2, 768], P(None, ('dp', 'seq'))
- grad_hidden_weight: float32 [2, 768, 3072], P(None, ('dp', 'seq'))
- grad_hidden_bias: float32 [2, 3072], P(None, ('dp', 'seq'))
- grad_proj_weight: float32 [2, 3072, 768], P(None, ('dp', 'seq'))
- grad_proj_bias: float32 [2, 768], P(None, ('dp', 'seq'))
The draws below stay inside these ranges and needn't reach their ends.
All inputs are finite; a program needn't handle non-finite values.
Results may differ from the reference program's by a relative error of at most 0.038.
Values may be sent and summed in bfloat16 or wider, within the bound.
No kernel may reach another device: no remote copies, remote signals or barrier semaphores. Data moves between devices by JAX's collectives and lax.ppermute only.
A program may use at most 256 MiB of HBM per device.

```python
import math
import jax
import jax.numpy as jnp
from jax import lax

D = 768
HEADS = 12
HEAD_DIM = 64
FF = 3072
LAYERS = 2
LEN = 1024
SEQS = 8


def block_levels(stream_key, extent, split, low, high):
    level, own = 1.0, jax.random.fold_in(stream_key, 6)
    for position, shards_of in split:
        heights = jnp.exp(jax.random.uniform(jax.random.fold_in(own, position), (shards_of,), jnp.float32, low / len(split), high / len(split)))
        level = level * jnp.repeat(heights, extent[position] // shards_of).reshape([-1 if axis == position else 1 for axis in range(len(extent))])
    return level


def centred(own_key, extent, scale, bound, shards=(), held_as=jnp.bfloat16):
    entries = scale * jax.random.normal(own_key, extent, jnp.float32)
    if shards:
        entries = entries * block_levels(own_key, extent, shards, -0.22, 0.18)
    return jnp.clip(entries, -bound, bound).astype(held_as)


def setup_inputs(seed: int = 0) -> dict:
    splits = jax.random.split(jax.random.key(seed), 18)
    return {
        "inputs": centred(splits[0], (SEQS, LEN, D), 1.0, 6.0, ((0, 8), (1, 4))),
        "cotangent": centred(splits[1], (SEQS, LEN, D), 1.0, 6.0, ((0, 8), (1, 4))),
        "norm1_gain": jnp.clip(1.0 + 0.1 * jax.random.normal(splits[2], (LAYERS, D), jnp.float32), 0.5, 1.5).astype(jnp.bfloat16),
        "norm1_shift": centred(splits[3], (LAYERS, D), 0.3, 3.0, ((1, 32),)),
        "query_weight": centred(splits[4], (LAYERS, D, D), D ** -0.5, 0.21875, ((1, 32),)),
        "query_bias": centred(splits[5], (LAYERS, D), 0.5, 3.0, ((1, 32),)),
        "key_weight": centred(splits[6], (LAYERS, D, D), D ** -0.5, 0.21875, ((1, 32),)),
        "value_weight": centred(splits[7], (LAYERS, D, D), D ** -0.5, 0.21875, ((1, 32),)),
        "value_bias": centred(splits[8], (LAYERS, D), 0.05, 0.75, ((1, 32),)),
        "out_weight": centred(splits[9], (LAYERS, D, D), (max(D // 256, 1)) ** -0.5, 3.5, ((1, 32),)),
        "out_bias": centred(splits[10], (LAYERS, D), 0.3, 3.0, ((1, 32),)),
        "norm2_gain": jnp.clip(1.0 + 0.1 * jax.random.normal(splits[11], (LAYERS, D), jnp.float32), 0.5, 1.5).astype(jnp.bfloat16),
        "norm2_shift": centred(splits[12], (LAYERS, D), 0.3, 3.0, ((1, 32),)),
        "hidden_weight": centred(splits[13], (LAYERS, D, FF), D ** -0.5, 0.21875, ((1, 32),)),
        "hidden_bias": centred(splits[14], (LAYERS, FF), 0.5, 3.0, ((1, 32),)),
        "proj_weight": centred(splits[15], (LAYERS, FF, D), FF ** -0.5, 0.109375, ((1, 32),)),
        "proj_bias": centred(splits[16], (LAYERS, D), 0.3, 3.0, ((1, 32),)),
    }


highest = lax.Precision.HIGHEST
epsilon = 1e-05

@jax.custom_vjp
def low(v):
    return lax.optimization_barrier(v.astype(jnp.bfloat16)).astype(jnp.float32)

@jax.custom_vjp
def low_back(v):
    return v

def low_keep(v):
    return (low(v), None)

def low_pass(kept, grad):
    return (grad,)

def back_keep(v):
    return (v, None)

def back_low(kept, grad):
    return (low(grad),)
low.defvjp(low_keep, low_pass)
low_back.defvjp(back_keep, back_low)

def norm_rows(values, norm_gain, norm_shift):
    center = values - lax.optimization_barrier(jnp.mean(values, axis=-1, keepdims=True))
    spread = lax.optimization_barrier(jnp.mean(center * center, axis=-1, keepdims=True))
    return center * lax.rsqrt(spread + epsilon) * norm_gain + norm_shift

def linear(left_side, weight):
    return jnp.einsum('btd,de->bte', left_side, weight, precision=highest)

def attend(queries, keys, values):
    block_size = min(512, LEN)
    block_count = LEN // block_size
    batch = queries.shape[0]
    heads_keys = keys.reshape(batch, LEN, HEADS, HEAD_DIM)
    heads_values = values.reshape(batch, LEN, HEADS, HEAD_DIM)
    blocks = queries.reshape(batch, block_count, block_size, HEADS, HEAD_DIM).transpose(1, 0, 2, 3, 4)

    def one_block(query_block):
        scores = jnp.einsum('bqhe,bkhe->bhqk', query_block, heads_keys, precision=highest) * (1.0 / math.sqrt(HEAD_DIM))
        scores = low_back(scores)
        probability = low(low_back(jax.nn.softmax(scores, axis=-1)))
        return jnp.einsum('bhqk,bkhe->bqhe', probability, heads_values, precision=highest)
    outcome = lax.map(jax.checkpoint(one_block), blocks)
    return outcome.transpose(1, 0, 2, 3, 4).reshape(queries.shape)

def layer_forward(hidden, weights):
    gain_one, shift_one, w_query, b_query, w_key, w_value, b_value, w_out, b_out, gain_two, shift_two, w_hidden, b_hidden, w_proj, b_proj = weights
    normed = low(norm_rows(hidden, gain_one, shift_one))
    queries = low(low_back(linear(normed, w_query) + b_query))
    keys = low(low_back(linear(normed, w_key)))
    values = low(low_back(linear(normed, w_value) + b_value))
    attended = low(low_back(attend(queries, keys, values)))
    middle = hidden + low_back(linear(attended, w_out) + b_out)
    normed_two = low(norm_rows(middle, gain_two, shift_two))
    preact = low_back(linear(normed_two, w_hidden) + b_hidden)
    active = low(jax.nn.gelu(preact, approximate=False))
    return middle + low_back(linear(active, w_proj) + b_proj)

def reference(inputs, cotangent, norm1_gain, norm1_shift, query_weight, query_bias, key_weight, value_weight, value_bias, out_weight, out_bias, norm2_gain, norm2_shift, hidden_weight, hidden_bias, proj_weight, proj_bias):
    params = tuple((member.astype(jnp.float32) for member in (norm1_gain, norm1_shift, query_weight, query_bias, key_weight, value_weight, value_bias, out_weight, out_bias, norm2_gain, norm2_shift, hidden_weight, hidden_bias, proj_weight, proj_bias)))

    def forward(clip_rows, weights):
        hidden = clip_rows[None]
        for layer_index in range(LAYERS):
            hidden = layer_forward(hidden, tuple((member[layer_index] for member in weights)))
        return hidden[0]

    def per_clip(totals, clip_pair):
        clip_rows, clip_cotangent = clip_pair
        result, pullback = jax.vjp(forward, clip_rows.astype(jnp.float32), params)
        grad_clip, grad_params = pullback(clip_cotangent.astype(jnp.float32))
        totals = jax.tree.map(lambda left_side, right_side: left_side + right_side, totals, grad_params)
        return (totals, (result.astype(jnp.bfloat16), grad_clip))
    zero_grads = jax.tree.map(jnp.zeros_like, params)
    totals, (outputs, grad_inputs) = lax.scan(per_clip, zero_grads, (inputs, cotangent))
    return (outputs, grad_inputs, totals[0], totals[1], totals[2], totals[3], totals[4], totals[5], totals[6], totals[7], totals[8], totals[9], totals[10], totals[11], totals[12], totals[13], totals[14])
```

```python
import math

import jax
import jax.numpy as jnp
import numpy as np
from jax import lax
from jax.experimental import pallas as pl
from jax.experimental.pallas import tpu as pltpu
from jax.sharding import PartitionSpec as P

HEADS = 12
HEAD_DIM = 64
PAIRS = HEADS // 2
LANES = 2 * HEAD_DIM
epsilon = 1e-05
SMALL = 128
SUMS = 256
VECTORS = 8
F32 = jnp.float32
BF16 = jnp.bfloat16
BOTH = ("dp", "seq")
SCALE = 1.0 / math.sqrt(HEAD_DIM)
VMEM_BYTES = 62 * 1024 * 1024


def mm(left_side, right_side):
    return lax.dot_general(
        left_side, right_side, (((1,), (0,)), ((), ())), preferred_element_type=F32
    )


def mm_nt(left_side, right_side):
    return lax.dot_general(
        left_side, right_side, (((1,), (1,)), ((), ())), preferred_element_type=F32
    )


def mm_tn(left_side, right_side):
    return lax.dot_general(
        left_side, right_side, (((0,), (0,)), ((), ())), preferred_element_type=F32
    )


def spread_matrix(ways):
    table = np.zeros((128 * ways, 128 * ways), np.float32)
    for source in range(128 * ways):
        table[source, (source % ways) * 128 + source // ways] = 1.0
    return jnp.asarray(table, BF16)


def deinterleave(values, ways):
    rows, columns = values.shape
    groups = columns // (128 * ways)
    moved = mm(values.reshape(rows * groups, 128 * ways), spread_matrix(ways)).astype(values.dtype)
    moved = moved.reshape(rows, groups, ways, 128)
    return moved.transpose(0, 2, 1, 3).reshape(rows, columns)


def norm_parts(values):
    center = values - jnp.mean(values, axis=-1, keepdims=True)
    spread = jnp.mean(center * center, axis=-1, keepdims=True)
    inverse = lax.rsqrt(spread + epsilon)
    return center * inverse, inverse


def norm_rows(values, gain, shift):
    return norm_parts(values)[0] * gain + shift


def norm_back(values, gain, gradient):
    unit, inverse = norm_parts(values)
    scaled = gradient * gain
    mean_plain = jnp.mean(scaled, axis=-1, keepdims=True)
    mean_unit = jnp.mean(scaled * unit, axis=-1, keepdims=True)
    by_values = inverse * (scaled - mean_plain - unit * mean_unit)
    by_gain = jnp.sum(gradient * unit, axis=0, keepdims=True)
    by_shift = jnp.sum(gradient, axis=0, keepdims=True)
    return by_values, by_gain, by_shift


def fetch(source, column, size, target, sem):
    return pltpu.make_async_copy(source.at[:, pl.ds(column, size)], target, sem)


def full(shape, dtype):
    return jax.ShapeDtypeStruct(shape, dtype)


LONG, SHORT = 100.0, 0.05
HINT = [SHORT]


def cost():
    micros = HINT[-1]
    return pl.CostEstimate(
        flops=int(micros * 1.1e9), transcendentals=0, bytes_accessed=int(micros * 3.0e6)
    )


def plain(builder, *operands):
    return builder(*operands)


def long(builder, *operands):
    HINT.append(LONG)
    try:
        return builder(*operands)
    finally:
        HINT.pop()


def call(name, kernel, operands, kept, outs, out_spaces, scratch, ahead):
    vmem = pl.BlockSpec(memory_space=pltpu.VMEM)
    away = pl.BlockSpec(memory_space=pl.ANY)
    ahead = [member for member in ahead if member is not None]
    read = len(operands)

    def used(*refs):
        kernel(*refs[:read], *refs[read + len(ahead) :])

    return pl.pallas_call(
        used,
        name=name,
        cost_estimate=cost(),
        out_shape=outs,
        in_specs=[away if far else vmem for far in kept] + [away] * len(ahead),
        out_specs=[away if far else vmem for far in out_spaces],
        scratch_shapes=scratch,
        compiler_params=pltpu.CompilerParams(vmem_limit_bytes=VMEM_BYTES),
    )(*operands, *ahead)


class Source:
    def __init__(self, arrays, plan=None, block=None):
        self.arrays = arrays
        self.plan = plan
        self.block = block

    def loads(self):
        return 1 if self.plan is None else len(self.plan)

    def load(self, refs, column, size, target, at, sems, first):
        copies = []
        if self.plan is None:
            copies.append(
                pltpu.make_async_copy(
                    refs[0].at[:, pl.ds(column, size)],
                    target.at[:, pl.ds(at, size)],
                    sems.at[first],
                )
            )
        else:
            me = lax.axis_index("dp")
            for number, (array, member, offset, row, count) in enumerate(self.plan):
                start = pl.multiple_of((me ^ offset) * self.block + row, 16)
                rows = refs[array] if member is None else refs[array].at[member]
                copies.append(
                    pltpu.make_async_copy(
                        rows.at[:, pl.ds(column, size)],
                        target.at[pl.ds(start, count), pl.ds(at, size)],
                        sems.at[first + number],
                    )
                )
        for copy in copies:
            copy.start()
        return copies


def wait_all(copies):
    for copy in copies:
        copy.wait()


def forward_qkv(layer, layers, ways, blocks, small, source, small_at, ahead):
    first = layer == 0
    frames, width = blocks[0].shape
    count = len(blocks)
    total = count * frames
    base = layer * (VECTORS + ways)
    sum_rows = -(-layers * (VECTORS + ways) // 8) * 8
    given = [] if first else [small]
    loads = source.loads()
    arrays = len(source.arrays)
    assemble = source.plan is not None

    def kernel(*refs):
        block_refs, refs = refs[:count], refs[count:]
        small_ref = None
        if not first:
            small_ref, *refs = refs
        source_refs, refs = refs[:arrays], refs[arrays:]
        q_out, k_out, v_out, a1_out, *refs = refs
        if first:
            small_ref, *refs = refs
        if assemble:
            weights_hbm, *refs = refs
        weights, sems, out_sem, *refs = refs
        if first:
            narrow = refs[0]
            narrow_copies = source.load(source_refs, small_at, SMALL, narrow, 0, sems, loads)
        copies = source.load(source_refs, 0, 3 * width, weights, 0, sems, 0)
        if first:
            wait_all(narrow_copies)
            small_ref[...] = narrow[...].astype(F32).T[:sum_rows]

        def vector(index):
            return small_ref[base + index : base + index + 1, :]

        for i in range(count):
            block = block_refs[i][...]
            if first:
                block = norm_rows(block.astype(F32), vector(0), vector(1)).astype(BF16)
            a1_out[i * frames : (i + 1) * frames, :] = block
        wait_all(copies)
        if assemble:
            assembled = pltpu.make_async_copy(weights, weights_hbm, out_sem.at[0])
            assembled.start()
        q_out[...] = (mm(a1_out[:frames, :], weights[:, :width]) + vector(2)).astype(BF16)
        k_out[...] = mm(a1_out[...], weights[:, width : 2 * width]).astype(BF16)
        v_out[...] = (mm(a1_out[...], weights[:, 2 * width :]) + vector(3)).astype(BF16)
        if assemble:
            assembled.wait()

    outs = [
        full((frames, width), BF16),
        full((total, width), BF16),
        full((total, width), BF16),
        full((total, width), BF16),
    ]
    spaces = [False] * 4
    scratch = [
        pltpu.VMEM((width, 3 * width), BF16),
        pltpu.SemaphoreType.DMA((2 * loads,)),
        pltpu.SemaphoreType.DMA((1,)),
    ]
    if first:
        outs.append(full((sum_rows, width), F32))
        spaces.append(False)
        scratch.append(pltpu.VMEM((width, SMALL), BF16))
    if assemble:
        outs.append(full((width, 3 * width), BF16))
        spaces.append(True)
    operands = [*blocks, *given, *source.arrays]
    far = [False] * (len(operands) - arrays) + [True] * arrays
    q, k, v, a1_full, *rest = call("forward_qkv", kernel, operands, far, outs, spaces, scratch, ahead)
    if first:
        small, *rest = rest
    return q, k, v, a1_full, small, rest[0] if assemble else source.arrays[0]


def both_heads(rows, low):
    zero = jnp.zeros_like(rows)
    return jnp.concatenate([jnp.where(low, rows, zero), jnp.where(low, zero, rows)], axis=0)


def forward_heads(q, k, v, ahead):
    frames, width = q.shape

    def kernel(q_ref, k_ref, v_ref, lse_out, o_out, lse_ref):
        lane = lax.broadcasted_iota(jnp.int32, (1, LANES), 1)
        low = lane < HEAD_DIM
        lse_ref[...] = jnp.zeros_like(lse_ref)

        def pair(index, carry):
            columns = pl.ds(pl.multiple_of(index * LANES, LANES), LANES)
            k2 = k_ref[:, columns]
            v2 = v_ref[:, columns]
            scores = mm_nt(both_heads(q_ref[:, columns] * SCALE, low), k2)
            top = jnp.max(scores, axis=-1, keepdims=True)
            exponent = jnp.exp(scores - top)
            sums = jnp.sum(exponent, axis=-1, keepdims=True)
            mixed = mm(exponent.astype(BF16), v2) * (1.0 / sums)
            lse_ref[...] = jnp.where(lane == index, top + jnp.log(sums), lse_ref[...])
            o_out[:, columns] = jnp.where(low, mixed[:frames], mixed[frames:]).astype(BF16)
            return carry

        lax.fori_loop(0, PAIRS, pair, 0)
        lse_out[...] = lse_ref[...].T[: lse_out.shape[0]]

    return call(
        "forward_heads",
        kernel,
        [q, k, v],
        [False] * 3,
        [full((8, 2 * frames), F32), full((frames, width), BF16)],
        [False] * 2,
        [pltpu.VMEM((2 * frames, LANES), F32)],
        ahead,
    )


def forward_mlp(layer, last, ways, own, o, small, source, at, ahead):
    frames, width = o.shape
    base = layer * (VECTORS + ways)
    loads = source.loads()
    arrays = len(source.arrays)
    assemble = source.plan is not None
    cuts = (0, (1 + ways) * width, (1 + 2 * ways) * width)

    def kernel(own_ref, o_ref, small_ref, *refs):
        source_refs, refs = refs[:arrays], refs[arrays:]
        h1_out, a2_out, g_out, slope_out, h_out, *refs = refs
        if not last:
            next_out, *refs = refs
        if assemble:
            weights_hbm, *refs = refs
        weights, sems, out_sem = refs
        copies = [
            source.load(
                source_refs,
                at + cuts[part],
                cuts[part + 1] - cuts[part],
                weights,
                cuts[part],
                sems,
                part * loads,
            )
            for part in range(2)
        ]

        def vector(index):
            return small_ref[base + index : base + index + 1, :]

        def weight(index):
            return weights[:, index * width : (index + 1) * width]

        hidden = own_ref[...].astype(F32) + vector(4)
        wait_all(copies[0])
        middle = hidden + mm(o_ref[...], weight(0))
        h1_out[...] = middle
        a2 = norm_rows(middle, vector(5), vector(6)).astype(BF16)
        a2_out[...] = a2
        following = middle + vector(7)
        for b in range(ways):
            u = mm(a2, weight(1 + b)) + vector(VECTORS + b)
            phi = 0.5 + 0.5 * lax.erf(u * math.sqrt(0.5))
            density = jnp.exp(-0.5 * u * u) * (1.0 / math.sqrt(2.0 * math.pi))
            g = (u * phi).astype(BF16)
            g_out[:, b * width : (b + 1) * width] = g
            slope_out[:, b * width : (b + 1) * width] = (phi + u * density).astype(BF16)
            if b == 0:
                wait_all(copies[1])
                if assemble:
                    assembled = pltpu.make_async_copy(weights, weights_hbm, out_sem.at[0])
                    assembled.start()
            following = following + mm(g, weight(1 + ways + b))
        h_out[...] = following.astype(h_out.dtype)
        if not last:
            up = base + VECTORS + ways
            next_out[...] = norm_rows(
                following, small_ref[up : up + 1, :], small_ref[up + 1 : up + 2, :]
            ).astype(BF16)
        if assemble:
            assembled.wait()

    row = (frames, width)
    outs = [
        full(row, F32),
        full(row, BF16),
        full((frames, ways * width), BF16),
        full((frames, ways * width), BF16),
        full(row, BF16 if last else F32),
    ]
    spaces = [False] * 5
    if not last:
        outs.append(full(row, BF16))
        spaces.append(False)
    if assemble:
        outs.append(full((width, cuts[2]), BF16))
        spaces.append(True)
    operands = [own, o, small, *source.arrays]
    h1, a2, g, slope, following, *rest = call(
        "forward_mlp",
        kernel,
        operands,
        [False] * 3 + [True] * arrays,
        outs,
        spaces,
        [
            pltpu.VMEM((width, cuts[2]), BF16),
            pltpu.SemaphoreType.DMA((2 * loads,)),
            pltpu.SemaphoreType.DMA((1,)),
        ],
        ahead,
    )
    a1_next = None
    if not last:
        a1_next, *rest = rest
    weights, weights_at = (rest[0], 0) if assemble else (source.arrays[0], at)
    return h1, a2, g, slope, following, a1_next, weights, weights_at


class Target:
    def __init__(self, width, columns, split):
        self.columns = columns
        self.split = split
        self.outs = [full((width, columns), BF16)]
        self.copies = 1
        if split:
            self.blocks = width // split // 2
            self.outs = [full((self.blocks, split, columns), BF16)] * 2
            self.copies = 2 * self.blocks

    def put(self, terms, refs, start, size, sems, first):
        part = pl.ds(start, size)
        copies = []
        if self.split:
            core = lax.axis_index("dp") & 1
            for which in range(2):
                for block in range(self.blocks):
                    row = pl.multiple_of((2 * block + (core ^ which)) * self.split, 16)
                    copies.append(
                        pltpu.make_async_copy(
                            terms.at[pl.ds(row, self.split), part],
                            refs[which].at[block, :, part],
                            sems.at[first + len(copies)],
                        )
                    )
        else:
            copies.append(
                pltpu.make_async_copy(terms.at[:, part], refs[0].at[:, part], sems.at[first])
            )
        for copy in copies:
            copy.start()
        return copies


def backward_mlp(layer, ways, above, small, sums, h1, a2, g, slope, mlp, mlp_at, split, ahead):
    last = len(above) == 1
    frames, width = h1.shape
    base = layer * (VECTORS + ways)
    up = base + VECTORS + ways
    target = Target(width, 2 * ways * width, split)

    def kernel(*refs):
        above_refs = refs[: len(above)]
        small_ref, sums_ref, h1_ref, a2_ref, g_ref, slope_ref, mlp_hbm = refs[
            len(above) : len(above) + 7
        ]
        refs = refs[len(above) + 7 :]
        target_refs, refs = refs[: len(target.outs)], refs[len(target.outs) :]
        dh1_out, sums_out, w_hidden, w_proj, grads, sems, out_sems = refs
        w_copies = []
        for b in range(ways):
            for part, held in ((1, w_proj), (0, w_hidden)):
                w_copies.append(
                    fetch(
                        mlp_hbm,
                        mlp_at + (part * ways + b) * width,
                        width,
                        held.at[b],
                        sems.at[part * ways + b],
                    )
                )
        for copy in w_copies:
            copy.start()
        sums_out[...] = sums_ref[...]
        if last:
            dh = above_refs[0][...].astype(F32)
        else:
            dh1_above, da1, h_above = above_refs[0], above_refs[1], above_refs[2]
            gradient = da1[...] + above_refs[3][0].astype(F32) + above_refs[4][...].astype(F32)
            part, by_gain, by_shift = norm_back(
                h_above[...], small_ref[up : up + 1, :], gradient
            )
            dh = dh1_above[...] + part
            sums_out[up : up + 1, :] = by_gain
            sums_out[up + 1 : up + 2, :] = by_shift
        dm = dh.astype(BF16)
        sums_out[base + 7 : base + 8, :] = jnp.sum(dm.astype(F32), axis=0, keepdims=True)
        a2_turned = a2_ref[...].T
        da2 = jnp.zeros((frames, width), F32)
        out_copies = []

        def put(index):
            out_copies.extend(
                target.put(
                    grads, target_refs, index * width, 2 * width, out_sems, len(out_copies)
                )
            )

        for b in range(ways):
            part = slice(b * width, (b + 1) * width)
            w_copies[2 * b].wait()
            dg = mm_nt(dm, w_proj[b])
            du = (dg * slope_ref[:, part].astype(F32)).astype(BF16)
            sums_out[base + VECTORS + b : base + VECTORS + b + 1, :] = jnp.sum(
                du.astype(F32), axis=0, keepdims=True
            )
            w_copies[2 * b + 1].wait()
            da2 = da2 + mm_nt(du, w_hidden[b])
            grads[:, part] = mm(a2_turned, du).astype(BF16)
            grads[:, (ways + b) * width : (ways + b + 1) * width] = mm_tn(
                g_ref[:, part], dm
            ).astype(BF16)
            if b % 2:
                put(b - 1)
                put(ways + b - 1)
        part, by_gain, by_shift = norm_back(h1_ref[...], small_ref[base + 5 : base + 6, :], da2)
        dh1_out[...] = dh + part
        sums_out[base + 5 : base + 6, :] = by_gain
        sums_out[base + 6 : base + 7, :] = by_shift
        wait_all(out_copies)

    operands = [*above, small, sums, h1, a2, g, slope, mlp]
    result = call(
        "backward_mlp",
        kernel,
        operands,
        [False] * (len(operands) - 1) + [True],
        target.outs + [full((frames, width), F32), full(sums.shape, F32)],
        [True] * len(target.outs) + [False, False],
        [
            pltpu.VMEM((ways, width, width), BF16),
            pltpu.VMEM((ways, width, width), BF16),
            pltpu.VMEM((width, 2 * ways * width), BF16),
            pltpu.SemaphoreType.DMA((2 * ways,)),
            pltpu.SemaphoreType.DMA((ways * target.copies,)),
        ],
        ahead,
    )
    return result[:-2], result[-2], result[-1]


def backward_attention(
    layer, ways, given, q, k, v, lse, raw, small, sums, w_qkv, w_out, out_at, pairs, before, ahead
):
    frames, width = q.shape
    total = k.shape[0]
    count = total // frames
    base = layer * (VECTORS + ways)
    start, stop = pairs
    opening = start == 0
    closing = stop == PAIRS
    columns_out = (stop - start) * LANES
    cuts = len(before) + 1

    def kernel(given_ref, q_ref, k_ref, v_ref, lse_ref, sums_ref, *refs):
        if opening:
            out_hbm, *refs = refs
        if closing:
            earlier, refs = refs[: 3 * (cuts - 1)], refs[3 * (cuts - 1) :]
            raw_refs, refs = refs[: len(raw)], refs[len(raw) :]
            qkv_hbm, *refs = refs
        dq_out, dk_out, dv_out, sums_out, *refs = refs
        sums_out[...] = sums_ref[...]
        if opening:
            dz_out, do_ref, *refs = refs
        else:
            do_ref = given_ref
        if closing:
            da_outs, refs = refs[:3], refs[3:]
            da_own, da_pair, da_cross = da_outs
            da_outs = [da_own, da_pair.at[0], da_cross, da_pair.at[1]]
        if opening:
            w_out_ref, sem, *refs = refs
            copy = fetch(out_hbm, out_at, width, w_out_ref, sem.at[0])
            copy.start()
        if closing:
            weights, sems, dq_all, dk_all, dv_all = refs
            copies = [
                fetch(qkv_hbm, i * width, width, weights.at[i], sems.at[i]) for i in range(3)
            ]
            for i in (1, 2, 0):
                copies[i].start()
        if opening:
            dz = given_ref[...].astype(BF16)
            dz_out[...] = dz
            sums_out[base + 4 : base + 5, :] = jnp.sum(dz.astype(F32), axis=0, keepdims=True)
            copy.wait()
            do_ref[...] = mm_nt(dz, w_out_ref[...]).astype(BF16)
        low = lax.broadcasted_iota(jnp.int32, (1, LANES), 1) < HEAD_DIM
        low_rows = lax.broadcasted_iota(jnp.int32, (LANES, 1), 0) < HEAD_DIM

        def pair(index, carry):
            columns = pl.ds(pl.multiple_of(index * LANES, LANES), LANES)
            target = pl.ds(pl.multiple_of((index - start) * LANES, LANES), LANES)
            q4 = both_heads(q_ref[:, columns] * SCALE, low)
            do4 = both_heads(do_ref[:, columns], low)
            k2 = k_ref[:, columns]
            p = jnp.exp(mm_nt(k2, q4) - lse_ref[pl.ds(index, 1), :])
            share = p * mm_nt(v_ref[:, columns], do4)
            inner = jnp.sum(share, axis=0, keepdims=True)
            ds = (share - p * inner).astype(BF16)
            dv2 = mm(p.astype(BF16), do4).astype(BF16)
            dk2 = mm(ds, q4).astype(BF16)
            turned = mm_tn(k2, ds)
            dq2 = jnp.where(low_rows, turned[:, :frames], turned[:, frames:]).T * SCALE
            dq_out[:, target] = dq2.astype(BF16)
            dk_out[:, target] = dk2
            dv_out[:, target] = dv2
            return carry

        lax.fori_loop(start, stop, pair, 0)
        if not closing:
            return
        at = 0
        for number in range(cuts):
            if number < cuts - 1:
                members = earlier[3 * number : 3 * number + 3]
            else:
                members = (dq_out, dk_out, dv_out)
            size = members[0].shape[1]
            for member, whole in zip(members, (dq_all, dk_all, dv_all)):
                whole[:, at : at + size] = member[...]
            at += size
        wait_all(copies)
        for i in range(count):
            rows = slice(i * frames, (i + 1) * frames)
            da = mm_nt(dk_all[rows, :], weights[1]) + mm_nt(dv_all[rows, :], weights[2])
            if i == 0:
                da = da + mm_nt(dq_all[...], weights[0])
                by_gain = jnp.zeros((1, width), F32)
                by_shift = jnp.zeros((1, width), F32)
            if raw:
                unit, _ = norm_parts(raw_refs[i][...].astype(F32))
                by_gain += jnp.sum(da * unit, axis=0, keepdims=True)
                by_shift += jnp.sum(da, axis=0, keepdims=True)
            da_outs[i][...] = da.astype(da_outs[i].dtype)
        if raw:
            sums_out[base : base + 1, :] = by_gain
            sums_out[base + 1 : base + 2, :] = by_shift
        sums_out[base + 2 : base + 3, :] = jnp.sum(dq_all[...].astype(F32), axis=0, keepdims=True)
        sums_out[base + 3 : base + 4, :] = jnp.sum(dv_all[...].astype(F32), axis=0, keepdims=True)

    row = (frames, width)
    outs = [
        full((frames, columns_out), BF16),
        full((total, columns_out), BF16),
        full((total, columns_out), BF16),
        full(sums.shape, F32),
    ]
    operands = [given, q, k, v, lse, sums]
    far = [False] * 6
    scratch = []
    if opening:
        outs += [full(row, BF16), full(row, BF16)]
        operands.append(w_out)
        far.append(True)
        scratch += [pltpu.VMEM((width, width), BF16), pltpu.SemaphoreType.DMA((1,))]
    if closing:
        outs += [full(row, F32), full((2,) + row, BF16), full(row, BF16)]
        extra = [member for part in before for member in part] + list(raw)
        operands += [*extra, w_qkv]
        far += [False] * len(extra) + [True]
        scratch += [
            pltpu.VMEM((3, width, width), BF16),
            pltpu.SemaphoreType.DMA((3,)),
            pltpu.VMEM(row, BF16),
            pltpu.VMEM((total, width), BF16),
            pltpu.VMEM((total, width), BF16),
        ]
    result = call(
        "backward_attention", kernel, operands, far, outs, [False] * len(outs), scratch, ahead
    )
    parts, sums, rest = list(result[:3]), result[3], list(result[4:])
    opened, rest = (rest[:2], rest[2:]) if opening else ([], rest)
    return parts, sums, opened, rest


def attention_grads(a1, o, dz, parts, sums, split, ahead):
    total, width = a1.shape
    frames = o.shape[0]
    columns = 4 * width + (SUMS if sums is not None else 0)
    extra = [] if sums is None else [sums]
    target = Target(width, columns, split)
    cuts = len(parts)

    def kernel(a1_ref, o_ref, dz_ref, *refs):
        part_refs, refs = refs[: 3 * cuts], refs[3 * cuts :]
        if extra:
            sums_ref, *refs = refs
        target_refs, refs = refs[: len(target.outs)], refs[len(target.outs) :]
        grads, turned, sems = refs
        copies = []

        def put(start, size):
            copies.extend(target.put(grads, target_refs, start, size, sems, len(copies)))

        if extra:
            table = sums_ref[...]
            table = jnp.concatenate(
                [table, jnp.zeros((128 - table.shape[0], width), F32)], axis=0
            )
            grads[:, 4 * width : 4 * width + 128] = table.T.astype(BF16)
            grads[:, 4 * width + 128 : columns] = jnp.zeros((width, SUMS - 128), BF16)
        grads[:, 3 * width : 4 * width] = mm(o_ref[...].T, dz_ref[...]).astype(BF16)
        put(3 * width, columns - 3 * width)
        turned[...] = a1_ref[...].T
        for index in range(3):
            column = index * width
            for number in range(cuts):
                ref = part_refs[3 * number + index]
                size = ref.shape[1]
                left = turned[:, :frames] if index == 0 else turned[...]
                grads[:, column : column + size] = mm(left, ref[...]).astype(BF16)
                column += size
            if index:
                put((0, 0, 2 * width)[index], (0, 2 * width, width)[index])
        wait_all(copies)

    operands = [a1, o, dz, *(member for part in parts for member in part), *extra]
    return call(
        "attention_grads",
        kernel,
        operands,
        [False] * len(operands),
        target.outs,
        [True] * len(target.outs),
        [
            pltpu.VMEM((width, columns), BF16),
            pltpu.VMEM((width, total), BF16),
            pltpu.SemaphoreType.DMA((3 * target.copies,)),
        ],
        ahead,
    )


def finish_rows(raw, dh1, small, parts, ahead):
    frames, width = dh1.shape

    def kernel(raw_ref, dh1_ref, small_ref, *refs):
        gradient = refs[0][...] + refs[1][0].astype(F32) + refs[2][...].astype(F32)
        part, _, _ = norm_back(raw_ref[...].astype(F32), small_ref[0:1, :], gradient)
        refs[-1][...] = (dh1_ref[...] + part).astype(BF16)

    operands = [raw, dh1, small, *parts]
    return call(
        "finish_rows",
        kernel,
        operands,
        [False] * len(operands),
        [full((frames, width), BF16)],
        [False],
        [],
        ahead,
    )[0]


def hold(values, column, columns, ahead):
    def kernel(source, target):
        target[...] = source[:, column : column + columns]

    outs = [full((values.shape[0], columns), values.dtype)]
    return call("hold", kernel, [values], [False], outs, [False], [], ahead)[0]


def join(members, ahead):
    count = len(members)

    def kernel(*refs):
        for index in range(count):
            refs[count][index] = refs[index][...]

    outs = [full((count,) + members[0].shape, members[0].dtype)]
    return call("join", kernel, members, [False] * count, outs, [False], [], ahead)[0]


def relay(base, first, second, ahead):
    rows, width = base.shape
    half = rows // 2

    def kernel(base_ref, first_ref, second_ref, upper_out, lower_out, joined):
        upper_out[...] = second_ref[:half, :]
        lower_out[...] = first_ref[half:, :]
        for index, ref in enumerate((base_ref, first_ref, second_ref)):
            joined[index] = ref[...]

    outs = [full((half, width), BF16)] * 2 + [full((3, rows, width), BF16)]
    return call(
        "relay", kernel, [base, first, second], [False] * 3, outs, [False] * 3, [], ahead
    )


def assemble(members, ahead):
    rows, width = members[0].shape
    count = len(members)

    def kernel(*refs):
        position = lax.axis_index("seq")
        for step in range(count):
            refs[count][position ^ step] = refs[step][...]

    outs = [full((count, rows, width), members[0].dtype)]
    whole = call("assemble", kernel, members, [False] * count, outs, [False], [], ahead)[0]
    return whole.reshape(count * rows, width)


def column_block(columns):
    for size in range(1664, 0, -128):
        if columns % size == 0:
            return size
    return columns


def add_halves(bits, kept, received, stage, ahead):
    if stage == 1:
        blocks, rows, columns = kept[0].shape
        cut = columns // 2
        lead = blocks // 2
    else:
        blocks, rows, cut = kept[0].shape
        lead = blocks // 2
    size = column_block(cut)
    steps = cut // size

    def where(right, sent):
        def index(block, column, own):
            x, y = own[1] ^ int(sent), own[2] ^ int(sent)
            if stage == 1:
                if right:
                    return (2 * y + block, 0, column + steps)
                return (2 * block + x, 0, column)
            return (x if right else y, 0, column)

        return index

    operands, in_specs = [], []
    for right in (False, True):
        for sent in (False, True):
            source = 0 if stage == 1 else int(right)
            for member in (kept[source], received[source]):
                operands.append(member)
                in_specs.append(pl.BlockSpec((1, rows, size), where(right, sent)))

    ahead = [member for member in ahead if member is not None]

    def kernel(own, *refs):
        outs = refs[8 + len(ahead) :]
        for number in range(4):
            outs[number][...] = (
                refs[2 * number][...].astype(F32) + refs[2 * number + 1][...].astype(F32)
            ).astype(BF16)

    out_spec = pl.BlockSpec((1, rows, size), lambda block, column, own: (block, 0, column))
    return pl.pallas_call(
        kernel,
        name="add_halves",
        cost_estimate=cost(),
        out_shape=[full((lead, rows, cut), BF16)] * 4,
        grid_spec=pltpu.PrefetchScalarGridSpec(
            num_scalar_prefetch=1,
            grid=(lead, steps),
            in_specs=in_specs + [pl.BlockSpec(memory_space=pl.ANY)] * len(ahead),
            out_specs=[out_spec] * 4,
        ),
        compiler_params=pltpu.CompilerParams(vmem_limit_bytes=VMEM_BYTES),
    )(bits, *operands, *ahead)


def add_rows(kept, received, parts, ahead):
    _, block, half = kept[0].shape
    rows = block // parts
    width = 2 * half

    def kernel(left, left_in, right, right_in, mine_out, other_out, total):
        total[:, :half] = left[0].astype(F32) + left_in[0].astype(F32)
        total[:, half:] = right[0].astype(F32) + right_in[0].astype(F32)
        low = lax.axis_index("seq") & 1
        for index in range(parts // 2):
            for out, which in ((mine_out, low), (other_out, 1 - low)):
                start = pl.multiple_of((2 * index + which) * rows, 8)
                out[index] = total[pl.ds(start, rows), :].astype(BF16)

    return call(
        "add_rows",
        kernel,
        [kept[0], received[0], kept[1], received[1]],
        [False] * 4,
        [full((parts // 2, rows, width), BF16)] * 2,
        [False] * 2,
        [pltpu.VMEM((block, width), F32)],
        ahead,
    )


def add_block(kept, received, ahead):
    _, block, half = kept[0].shape

    def kernel(left, left_in, right, right_in, out):
        out[:, :half] = (left[0].astype(F32) + left_in[0].astype(F32)).astype(BF16)
        out[:, half:] = (right[0].astype(F32) + right_in[0].astype(F32)).astype(BF16)

    operands = [kept[0], received[0], kept[1], received[1]]
    outs = [full((block, 2 * half), BF16)]
    return call("add_block", kernel, operands, [False] * 4, outs, [False], [], ahead)[0]


def add_ends(kept, received, ahead):
    _, rows, width = kept.shape

    def kernel(kept_ref, received_ref, mine_out, other_out):
        high = lax.axis_index("seq") >> 1
        for out, which in ((mine_out, high), (other_out, 1 - high)):
            out[...] = (
                kept_ref[which].astype(F32) + received_ref[which].astype(F32)
            ).astype(BF16)

    return call(
        "add_ends",
        kernel,
        [kept, received],
        [False] * 2,
        [full((rows, width), BF16)] * 2,
        [False] * 2,
        [],
        ahead,
    )


def add_cross(kept, received, ahead):
    def kernel(kept_ref, received_ref, out):
        out[...] = (kept_ref[...].astype(F32) + received_ref[1].astype(F32)).astype(BF16)

    outs = [full(kept.shape, BF16)]
    return call(
        "add_cross", kernel, [kept, received], [False] * 2, outs, [False], [], ahead
    )[0]


def add_parts(members, ahead):
    def kernel(*refs):
        refs[-1][...] = total_of(refs[:-1], slice(None))

    outs = [full(members[0].shape, F32)]
    return call("add_parts", kernel, members, [False] * len(members), outs, [False], [], ahead)[0]


def total_of(refs, columns):
    value = refs[0][:, columns].astype(F32)
    for ref in refs[1:]:
        value = value + ref[:, columns].astype(F32)
    return value


def finish_mlp(layers, table, ways, ahead):
    rows, columns = layers[0][0].shape
    half = columns // 2
    counts = [len(members) for members in layers]
    width = half // ways

    def kernel(table_ref, *refs):
        hidden_out, proj_out = refs[sum(counts) :]
        row = lax.broadcasted_iota(jnp.int32, (rows * ways, rows * ways), 0)
        column = lax.broadcasted_iota(jnp.int32, (rows * ways, rows * ways), 1)
        turn = jnp.where(row == ways * (column % rows) + column // rows, 1.0, 0.0).astype(BF16)
        at = 0
        for layer, count in enumerate(counts):
            members = refs[at : at + count]
            at += count
            proj = jnp.concatenate(
                [
                    total_of(members, slice(half + b * width, half + (b + 1) * width))
                    for b in range(ways)
                ],
                axis=0,
            )
            proj_out[layer] = mm(turn, proj.astype(BF16))
            hidden = total_of(members, slice(0, half)).astype(BF16)
            for start in range(0, width, 128):
                group = jnp.concatenate(
                    [hidden[:, b * width + start : b * width + start + 128] for b in range(ways)],
                    axis=1,
                )
                hidden_out[layer, :, ways * start : ways * (start + 128)] = mm_nt(
                    group, table_ref[...]
                )

    operands = [table] + [member for members in layers for member in members]
    outs = [
        full((len(layers), rows, half), F32),
        full((len(layers), rows * ways, width), F32),
    ]
    return call(
        "finish_mlp", kernel, operands, [False] * len(operands), outs, [False] * 2, [], ahead
    )


def finish_attention(layers, ways, ahead):
    rows, columns = layers[0][0].shape
    counts = [len(members) for members in layers]
    width = (columns - SUMS) // 4
    each = VECTORS + ways

    def kernel(*refs):
        outs = refs[sum(counts) :]
        at = 0
        for layer, count in enumerate(counts):
            members = refs[at : at + count]
            at += count
            for index in range(4):
                outs[index][layer] = total_of(
                    members, slice(index * width, (index + 1) * width)
                )
            if layer == 0:
                sums = total_of(members, slice(4 * width, 4 * width + 128)).T
        for layer in range(len(counts)):
            for index in range(VECTORS):
                row = layer * each + index
                outs[4 + index][layer : layer + 1, :] = sums[row : row + 1, :]
            row = layer * each + VECTORS
            outs[4 + VECTORS][layer] = sums[row : row + ways, :]

    operands = [member for members in layers for member in members]
    count = len(layers)
    outs = [full((count, rows, width), F32)] * 4 + [full((count, rows), F32)] * VECTORS
    outs.append(full((count, ways, rows), F32))
    result = call(
        "finish_attention",
        kernel,
        operands,
        [False] * len(operands),
        outs,
        [False] * len(outs),
        [],
        ahead,
    )
    return result[:4], result[4:-1], result[-1]


def body(inputs, cotangent, *parameters):
    (
        norm1_gain,
        norm1_shift,
        query_weight,
        query_bias,
        key_weight,
        value_weight,
        value_bias,
        out_weight,
        out_bias,
        norm2_gain,
        norm2_shift,
        hidden_weight,
        hidden_bias,
        proj_weight,
        proj_bias,
    ) = parameters
    layers, rows, width = query_weight.shape
    ways = proj_weight.shape[1] // rows
    frames = inputs.shape[1]
    groups = lax.axis_size("dp")
    parts = lax.axis_size("seq")
    half = parts // 2
    group = lax.axis_index("dp")
    position = lax.axis_index("seq")

    def place(base, clip, quarter):
        return (2 * base + quarter % 2) * parts + clip * half + quarter // 2

    def home(base, clip, quarter):
        return (2 * base + clip) * parts + quarter

    spots = [
        (base, clip, quarter)
        for base in range(groups // 2)
        for clip in range(2)
        for quarter in range(parts)
    ]
    leave = [(home(*spot), place(*spot)) for spot in spots]
    back = [(target, source) for source, target in leave]

    def partner(values, step):
        pairs = [
            (place(base, clip, quarter), place(base, clip, quarter ^ step))
            for base, clip, quarter in spots
        ]
        return lax.ppermute(values, BOTH, pairs)

    def spread(values):
        if parts != 4:
            return [values] + [partner(values, step) for step in range(1, parts)]
        across_chips = partner(values, 2)
        return [values, partner(values, 1), across_chips, partner(across_chips, 1)]

    columns = []
    for layer in range(layers):
        for member in (
            norm1_gain,
            norm1_shift,
            query_bias,
            value_bias,
            out_bias,
            norm2_gain,
            norm2_shift,
            proj_bias,
        ):
            columns.append(member[layer].reshape(rows, 1))
        columns.append(hidden_bias[layer].reshape(rows, ways))
    used = layers * (VECTORS + ways)
    columns.append(jnp.zeros((rows, SMALL - used), BF16))
    sum_rows = -(-used // 8) * 8
    attn_packed, mlp_packed = [], []
    for layer in range(layers):
        members = [
            query_weight[layer],
            key_weight[layer],
            value_weight[layer],
        ]
        if layer == 0:
            members += columns
        attn_packed.append(jnp.concatenate(members, axis=1))
        mlp_packed.append(
            jnp.concatenate(
                [
                    out_weight[layer],
                    deinterleave(hidden_weight[layer], ways),
                    proj_weight[layer].reshape(rows, ways * width),
                ],
                axis=1,
            )
        )
    small_at = 3 * width

    block = parts * rows
    direct = groups == 8 and parts == 4 and layers == 2 and block % 32 == 0 and rows % 8 == 0
    own_bits = jnp.stack([(group >> bit) & 1 for bit in range(3)]).astype(jnp.int32)

    def exchange(values, flip):
        pairs = [(device, device ^ flip) for device in range(groups * parts)]
        return lax.ppermute(values, BOTH, pairs)

    core, across, along = parts, 2 * parts, 4 * parts

    class Gather:
        def __init__(self, base, column, columns):
            self.base = base
            self.place = (column, columns)

        def start(self, whole=False):
            self.near = [self.base, exchange(self.base, across), exchange(self.base, along)]
            if whole:
                self.near.append(exchange(self.base, across + along))

        def finish(self, ahead=()):
            upper, lower, joined = relay(*self.near, ahead)
            self.sends = [upper, lower]
            self.near += [exchange(upper, across), exchange(lower, along)]
            self.far = [exchange(joined, core)]

        def close(self, ahead=()):
            self.far.append(exchange(join(self.near[3:], ahead), core))

        def gather(self, ahead=()):
            self.joined = [join(self.near[:2], ahead), join(self.near[2:], ahead)]

        def source(self):
            plan = [(index, None, 2 * index, 0, block) for index in range(3)]
            if len(self.near) == 4:
                far = [exchange(member, core) for member in self.joined]
                plan.append((3, None, 6, 0, block))
                plan += [
                    (4 + index // 2, index % 2, 2 * index + 1, 0, block) for index in range(4)
                ]
                return Source(self.near + far, plan, block)
            half = block // 2
            plan += [(3 + index, None, 6, index * half, half) for index in range(2)]
            plan += [(5, index, 2 * index + 1, 0, block) for index in range(3)]
            plan += [(6, index, 7, index * half, half) for index in range(2)]
            return Source(self.near + self.far, plan, block)

    def gather_layer(layer):
        shard = jnp.concatenate([attn_packed[layer], mlp_packed[layer]], axis=1)
        return lax.all_gather(shard, BOTH, axis=0, tiled=True)

    queue = []
    if direct:
        shards = [shard for pair in zip(attn_packed, mlp_packed) for shard in pair]
        sizes = [shard.shape[1] for shard in shards]
        members = [shards[0]] + [exchange(shards[0], step) for step in range(1, parts)]
        queue = [Gather(assemble(members, ()), 0, sizes[0])]
        rows_two = lax.all_gather(shards[1], "seq", axis=0, tiled=True)
        queue.append(Gather(rows_two, 0, sizes[1]))
        queue[0].start(True)
        queue[0].gather()
        later = hold(jnp.concatenate(shards[2:], axis=1), 0, sum(sizes[2:]), [queue[0].base])
        later = lax.all_gather(later, "seq", axis=0, tiled=True)
        queue += [Gather(later, 0, sizes[2]), Gather(later, sizes[2], sizes[3])]
    else:
        gathered = [gather_layer(layer) for layer in range(layers)]
    raw = lax.ppermute(inputs.reshape(frames, width), BOTH, leave)
    raw_blocks = spread(raw)

    def follow(part, ahead, whole=False):
        part.base = long(hold, part.base, *part.place, ahead)
        part.start(whole)
        return [part.base]

    own, blocks, saved, small = raw, raw_blocks, [], None
    for layer in range(layers):
        last = layer == layers - 1
        mlp_at = attn_packed[layer].shape[1]
        source = queue[2 * layer].source() if direct else Source([gathered[layer]])
        ahead = []
        if direct:
            present = queue[2 * layer + 1]
            ahead = follow(present, []) if layer == 0 else [present.base]
        q, k, v, a1_full, small, w_qkv = (long if layer == 0 else plain)(
            forward_qkv, layer, layers, ways, blocks, small, source, small_at, ahead
        )
        ahead = []
        if direct and layer > 0:
            present.finish([q])
            ahead = present.sends
        lse, o = (plain if layer == 0 else long)(forward_heads, q, k, v, ahead)
        ahead = []
        if direct:
            if layer == 0:
                present.finish([lse])
            present.close([lse])
            source, mlp_at = present.source(), 0
            if not last:
                ahead = follow(queue[2 * layer + 2], present.near[3:], True)
                ahead += follow(queue[2 * layer + 3], ahead)
        h1, a2, g, slope, following, a1_next, w_mlp, mlp_at = long(
            forward_mlp, layer, last, ways, own, o, small, source, mlp_at, ahead
        )
        w_out, out_at, mlp_at = w_mlp, mlp_at, mlp_at + width
        coming = [] if last else spread(a1_next)
        if direct and not last:
            queue[2 * layer + 2].gather([a1_next])
        if layer == 0:
            top = hold(cotangent.reshape(frames, width), 0, width, [a2])
            top = lax.ppermute(top, BOTH, leave)
        saved.append(
            (
                own,
                a1_full,
                q,
                k,
                v,
                lse,
                o,
                h1,
                a2,
                g,
                slope,
                w_qkv,
                w_out,
                out_at,
                w_mlp,
                mlp_at,
            )
        )
        own = following
        blocks = coming
    final = lax.ppermute(own, BOTH, back)

    class Chain:
        def __init__(self, terms, beside=False):
            self.beside = beside
            self.stage = 0 if len(terms) == 2 else 4
            self.total = None
            if len(terms) == 2:
                self.kept = [terms[0]]
                self.received = [exchange(terms[1], core)]
            else:
                self.total = lax.psum_scatter(
                    terms[0], BOTH, scatter_dimension=0, tiled=True
                ).astype(F32)

        def step(self, ahead=()):
            self.stage += 1
            if self.stage < 3:
                left, left_send, right, right_send = add_halves(
                    own_bits, self.kept, self.received, self.stage, ahead
                )
                turns = (across, along) if self.stage == 1 else (along, across)
                self.kept = [left, right]
                self.received = [exchange(left_send, turns[0]), exchange(right_send, turns[1])]
                return [left_send, right_send]
            if self.stage == 3 and self.beside:
                block_terms = add_block(self.kept, self.received, ahead)
                self.kept, self.received = [
                    lax.psum_scatter(block_terms, "seq", scatter_dimension=0, tiled=True)
                ], []
                self.stage = 4
                return [block_terms]
            if self.stage == 3:
                mine, send = add_rows(self.kept, self.received, parts, ahead)
                self.kept, self.received = [mine], [exchange(send, 1)]
            else:
                mine, send = add_ends(self.kept[0], self.received[0], ahead)
                self.kept, self.received = [mine], [exchange(send, 2)]
            return [send]

        def members(self):
            return self.kept + self.received if self.total is None else [self.total]

    split = block if direct else 0
    sums = jnp.zeros((sum_rows, width), F32)
    above = [top]
    mlp_chains, attn_chains = [None] * layers, [None] * layers
    done = []

    def steps(*chains):
        nonlocal done
        for chain in chains:
            if chain is not None and chain.stage < 4:
                done = [*chain.step(done), *done[:1]]

    def close(chain):
        nonlocal done
        if chain is not None and chain.total is None:
            while chain.stage < 4:
                steps(chain)
            chain.total = add_parts(chain.kept + chain.received, done)
            done = [chain.total]

    middle = HEADS // 4
    for layer in reversed(range(layers)):
        (
            own,
            a1_full,
            q,
            k,
            v,
            lse,
            o,
            h1,
            a2,
            g,
            slope,
            w_qkv,
            w_out,
            out_at,
            w_mlp,
            mlp_at,
        ) = saved[layer]
        upper_attn = None if layer == layers - 1 else attn_chains[layer + 1]
        upper_mlp = None if layer == layers - 1 else mlp_chains[layer + 1]
        terms, dh1, sums = long(
            backward_mlp,
            layer,
            ways,
            above,
            small,
            sums,
            h1,
            a2,
            g,
            slope,
            w_mlp,
            mlp_at,
            split,
            done,
        )
        mlp_chains[layer] = Chain(terms, layer > 0)
        done = list(terms[-1:])
        if layer == layers - 1:
            done.append(final)
        steps(upper_attn)
        before = []
        given, dz = dh1, None
        for pairs in ((0, middle), (middle, PAIRS)):
            part, sums, opened, da = long(
                backward_attention,
                layer,
                ways,
                given,
                q,
                k,
                v,
                lse,
                raw_blocks if layer == 0 else [],
                small,
                sums,
                w_qkv,
                w_out,
                out_at,
                pairs,
                before,
                done,
            )
            before = before + [part]
            if opened:
                dz, given = opened
            done = [sums]
            if not da:
                steps(mlp_chains[layer], upper_attn, upper_mlp)
        siblings = partner(da[1], 1)

        def cross():
            nonlocal done
            crossing = add_cross(da[2], siblings, done)
            done = [crossing]
            return partner(crossing, 2)

        if layer > 0:
            crossed = cross()
        else:
            steps(mlp_chains[layer], upper_attn)
            close(upper_mlp)
        terms = attention_grads(
            a1_full,
            o,
            dz,
            before,
            sums if layer == 0 else None,
            split,
            done,
        )
        attn_chains[layer] = Chain(terms)
        done = list(terms[-1:])
        if layer > 0:
            steps(mlp_chains[layer])
        else:
            steps(upper_attn)
            long(steps, mlp_chains[layer])
            crossed = cross()
            steps(attn_chains[layer])
        above = [dh1, da[0], own, siblings, crossed]
    grad_rows = long(finish_rows, raw, above[0], small, [above[1], *above[3:]], done)
    done = [grad_rows]
    grad_rows = lax.ppermute(grad_rows, BOTH, back).astype(F32)
    steps(attn_chains[0], mlp_chains[0], attn_chains[0])
    for chain in attn_chains[1:]:
        close(chain)
    steps(attn_chains[0])
    for chain in attn_chains + mlp_chains:
        while chain.stage < 4:
            steps(chain)
    table = spread_matrix(ways)
    grad_hidden, grad_proj = finish_mlp(
        [chain.members() for chain in mlp_chains], table, ways, done
    )
    weights, vectors, biases = finish_attention(
        [chain.members() for chain in attn_chains], ways, [grad_hidden]
    )
    grad_hbias = biases.transpose(0, 2, 1).reshape(layers, rows * ways)
    return (
        final.reshape(inputs.shape),
        grad_rows.reshape(inputs.shape),
        vectors[0],
        vectors[1],
        weights[0],
        vectors[2],
        weights[1],
        weights[2],
        vectors[3],
        weights[3],
        vectors[4],
        vectors[5],
        vectors[6],
        grad_hidden,
        grad_hbias,
        grad_proj,
        vectors[7],
    )


def solution(mesh):
    rows = P("dp", "seq", None)
    vector = P(None, BOTH)
    matrix = P(None, BOTH, None)
    params = (
        vector,
        vector,
        matrix,
        vector,
        matrix,
        matrix,
        vector,
        matrix,
        vector,
        vector,
        vector,
        matrix,
        vector,
        matrix,
        vector,
    )
    return jax.shard_map(
        body,
        mesh=mesh,
        in_specs=(rows, rows) + params,
        out_specs=(rows, rows) + params,
        check_vma=False,
    )
```
